32 devices in a mesh: section: 4 (over y, x), slab: 8 (over z, core).
Axes of the slice: x: 2, y: 2, z: 4, core: 2. Of those that a mesh axis runs over, the one named last changes fastest.
Arguments:
- ref_scan: float32 [256, 256, 512], P('slab', None, 'section'), may hold values from 0.03 to 10, as said below
- def_scan: float32 [256, 256, 512], P('slab', None, 'section'), may hold values from 0.03 to 10, as said below
- offsets: int32 [3, 3, 8, 8, 16], P(None, None, None, None, 'section'), may hold values from -224 to 224, as said below
Outputs:
- subset_shift: float32 [3, 8, 8, 16], P(None, 'slab', None, 'section')
- correlation: float32 [8, 8, 16], P('slab', None, 'section')
- crosslink: float32 [8, 8, 16], P('slab', None, 'section')
The draws below stay inside these ranges and needn't reach their ends.
Inputs may be any that keep to these rules, and one draw needn't show every extreme that they name: `ref_scan`: positive intensities. `def_scan`: positive intensities. offsets[k, :, s] is subset s's displacement in iteration k, in cells; the cube it points to lies inside the volume; the second and third components lie within -2..2; the slab in which the cube starts, (i * 32 + offsets[k, 0, s]) // 32, is the same in every iteration, and a cube that starts in the last slab starts at its first plane; of the subsets of one device, at most 4 start their cubes in one slab, and exactly 4 do in some slab.
All inputs are finite; a program needn't handle non-finite values.
Results may differ from the reference program's by a relative error of at most 0.0003.
Values may be sent and summed in bfloat16 or wider, within the bound.
A program may use at most 256 MiB of HBM per device.

```python
import math
import jax
import jax.numpy as jnp
from jax import lax

SUB = 32
RIM = 4
JIT = 2
ITERS = 3
NY = 256
NXD = 128
NZ = 256
NX = 512
CAP = 4


def layout(key):
    slab_count = NZ // SUB
    rows_sub = NY // SUB
    cols_sub = NX // SUB
    cols_dev = NXD // SUB
    groups = NX // NXD
    per_dev = rows_sub * cols_dev

    def one_group(group_key):
        key_list = jax.random.split(group_key, 4)
        order_pos = jax.random.permutation(key_list[0], per_dev)
        shift_base = jax.random.randint(key_list[1], (), 0, min(per_dev - CAP, slab_count - 1))
        slot_group = jnp.where(order_pos < CAP, 0, 1 + ((order_pos - CAP) * (slab_count - 1) + shift_base) // (per_dev - CAP))
        outer_perm = jax.random.permutation(key_list[2], slab_count)
        inner_perm = jax.random.permutation(key_list[3], slab_count)
        mixed_idx = (inner_perm[:, None] + slot_group[None, :]) % slab_count
        return outer_perm[mixed_idx]
    owners = jax.vmap(one_group)(jax.random.split(jax.random.fold_in(key, 7), groups))
    owners = owners.reshape(groups, slab_count, rows_sub, cols_dev).transpose(1, 2, 0, 3).reshape(slab_count, rows_sub, cols_sub)
    plane_off = jax.random.randint(jax.random.fold_in(key, 11), (rows_sub, cols_sub), JIT, SUB - JIT)
    wobble = jax.random.randint(jax.random.fold_in(key, 13), (ITERS, 3, slab_count, rows_sub, cols_sub), -JIT, JIT + 1)
    return (owners.astype(jnp.int32), plane_off.astype(jnp.int32), wobble.astype(jnp.int32))


def scan_ref(key):
    key_list = jax.random.split(jax.random.fold_in(key, 21), 3)
    periods = jax.random.uniform(key_list[0], (3,), jnp.float32, 48.0, 160.0)
    phase_off = jax.random.uniform(key_list[1], (), jnp.float32, 0.0, 2.0 * math.pi)
    depth = jnp.arange(NZ, dtype=jnp.float32)[:, None, None]
    height = jnp.arange(NY, dtype=jnp.float32)[None, :, None]
    across = jnp.arange(NX, dtype=jnp.float32)[None, None, :]
    wave_val = jnp.sin(2.0 * math.pi * (depth / periods[0] + height / periods[1] + across / periods[2]) + phase_off)
    grain_val = jax.random.uniform(key_list[2], (NZ, NY, NX), jnp.float32, 0.3, 1.7)
    return jnp.exp(0.5 * wave_val) * grain_val


def widen_cols(coarse):
    return jnp.repeat(jnp.repeat(coarse, SUB, axis=-2), SUB, axis=-1)


def draw_ref_scan(key, part):
    return scan_ref(key)


def draw_def_scan(key, part):
    source = scan_ref(key)
    owners, plane_off, wobble = layout(key)
    rows_sub = NY // SUB
    cols_sub = NX // SUB
    back_map = jnp.argsort(owners, axis=0).astype(jnp.int32)
    cell_back = widen_cols(back_map)
    cell_off = widen_cols(plane_off)
    fraction = widen_cols(jax.random.uniform(jax.random.fold_in(key, 31), (rows_sub, cols_sub), jnp.float32, 0.0, 1.0))
    dilute = widen_cols(jax.random.uniform(jax.random.fold_in(key, 33), (rows_sub, cols_sub), jnp.float32, 0.3, 0.8))
    depth = jnp.arange(NZ, dtype=jnp.int32)[:, None, None]

    def pulled(extra_plane):
        wrapped = (depth - cell_off[None] - extra_plane) % NZ
        anchor = jnp.take_along_axis(cell_back, wrapped // SUB, axis=0) * SUB + wrapped % SUB
        return jnp.take_along_axis(source, anchor, axis=0)
    blended = (1.0 - fraction) * pulled(0) + fraction * pulled(1)
    noise_val = jax.random.uniform(jax.random.fold_in(key, 35), (NZ, NY, NX), jnp.float32, 0.0, 0.1)
    return dilute * blended + noise_val


def draw_offsets(key, part):
    owners, plane_off, wobble = layout(key)
    slab_count, rows_sub, cols_sub = owners.shape
    last_slab = owners == slab_count - 1
    z_first = owners[None] * SUB + jnp.where(last_slab[None], 0, plane_off[None, None] + wobble[:, 0])
    z_move = z_first - (jnp.arange(slab_count, dtype=jnp.int32) * SUB)[None, :, None, None]
    row_home = (jnp.arange(rows_sub, dtype=jnp.int32) * SUB)[None, None, :, None]
    y_move = jnp.clip(row_home + wobble[:, 1], 0, NY - SUB) - row_home
    col_home = (jnp.arange(cols_sub, dtype=jnp.int32) * SUB)[None, None, None, :]
    x_move = jnp.clip(col_home + wobble[:, 2], 0, NX - SUB) - col_home
    return jnp.stack([z_move, y_move, x_move], axis=1).astype(jnp.int32)


def setup_inputs(seed: int = 0) -> dict:
    seeds = jax.random.split(jax.random.key(seed), 4)
    ref_scan = draw_ref_scan(jax.random.fold_in(seeds[3], 71), 0)
    def_scan = draw_def_scan(jax.random.fold_in(seeds[3], 71), 0)
    offsets = draw_offsets(jax.random.fold_in(seeds[3], 71), 0)
    return {"ref_scan": ref_scan, "def_scan": def_scan, "offsets": offsets}


def tap_tables():
    spots = [float(t) for t in range(-RIM, RIM + 1)]
    bell_curve = [math.exp(-t * t / 4.5) for t in spots]
    bell_total = sum(bell_curve)
    slope_norm = sum([t * t * b for t, b in zip(spots, bell_curve)])
    smooth = [b / bell_total for b in bell_curve]
    slope = [t * b / slope_norm for t, b in zip(spots, bell_curve)]
    return (smooth, slope)

def tap_sum(padded, weights, which_axis, length):
    running = weights[0] * lax.slice_in_dim(padded, 0, length, axis=which_axis)
    for tap_index in range(1, len(weights)):
        running = running + weights[tap_index] * lax.slice_in_dim(padded, tap_index, tap_index + length, axis=which_axis)
    return running

def zero_pad(values, which_axis):
    widths = [(0, 0)] * values.ndim
    widths[which_axis] = (RIM, RIM)
    return jnp.pad(values, widths)

def filtered(values, weights, which_axis):
    return tap_sum(zero_pad(values, which_axis), weights, which_axis, values.shape[which_axis])

def solve_three(k_mat, rhs_vec):
    k_zz, k_zy, k_zx = (k_mat[0][0], k_mat[0][1], k_mat[0][2])
    k_yy, k_yx, k_xx = (k_mat[1][1], k_mat[1][2], k_mat[2][2])
    c_zz = k_yy * k_xx - k_yx * k_yx
    c_zy = k_zx * k_yx - k_zy * k_xx
    c_zx = k_zy * k_yx - k_yy * k_zx
    c_yy = k_zz * k_xx - k_zx * k_zx
    c_yx = k_zy * k_zx - k_zz * k_yx
    c_xx = k_zz * k_yy - k_zy * k_zy
    determ = k_zz * c_zz + k_zy * c_zy + k_zx * c_zx
    return [(c_zz * rhs_vec[0] + c_zy * rhs_vec[1] + c_zx * rhs_vec[2]) / determ, (c_zy * rhs_vec[0] + c_yy * rhs_vec[1] + c_yx * rhs_vec[2]) / determ, (c_zx * rhs_vec[0] + c_yx * rhs_vec[1] + c_xx * rhs_vec[2]) / determ]

def spread_of(centred_sq, cross_vec, k_mat, along, volume):
    square = centred_sq
    for index_a in range(3):
        square = square + 2.0 * cross_vec[index_a] * along[index_a]
        for index_b in range(3):
            square = square + along[index_a] * k_mat[index_a][index_b] * along[index_b]
    return jnp.sqrt(square + 1e-06 * volume)

def gauss_newton(gram_mat, current):
    volume = gram_mat[..., 0, 0]
    mean_val = gram_mat[..., 0, 2] / volume
    mean_grad = [gram_mat[..., 0, 3 + index_a] / volume for index_a in range(3)]
    centred_sq = gram_mat[..., 2, 2] - volume * mean_val * mean_val
    cross_vec = [gram_mat[..., 2, 3 + index_a] - volume * mean_val * mean_grad[index_a] for index_a in range(3)]
    k_mat = [[gram_mat[..., 3 + index_a, 3 + index_b] - volume * mean_grad[index_a] * mean_grad[index_b] + (1e-06 * volume if index_a == index_b else 0.0) for index_b in range(3)] for index_a in range(3)]
    ref_grad = [gram_mat[..., 1, 3 + index_a] - mean_grad[index_a] * gram_mat[..., 0, 1] for index_a in range(3)]
    spread_now = spread_of(centred_sq, cross_vec, k_mat, current, volume)
    first_part = solve_three(k_mat, ref_grad)
    second_part = solve_three(k_mat, cross_vec)
    newest = [spread_now * first_part[index_a] - second_part[index_a] for index_a in range(3)]
    return (newest, (mean_val, centred_sq, cross_vec, k_mat, ref_grad, volume))

def finish(gram_mat, newest, moment_set, ref_mean):
    mean_val, centred_sq, cross_vec, k_mat, ref_grad, volume = moment_set
    spread_new = spread_of(centred_sq, cross_vec, k_mat, newest, volume)
    score_sum = gram_mat[..., 1, 2] - mean_val * gram_mat[..., 0, 1]
    for index_a in range(3):
        score_sum = score_sum + ref_grad[index_a] * newest[index_a]
    correlation = score_sum / spread_new
    polymer = mean_val / (mean_val + ref_mean)
    crosslink = -1000.0 * (jnp.log(1.0 - polymer) + polymer + 0.4 * polymer * polymer) / (106.3 * (jnp.cbrt(polymer) - 0.5 * polymer))
    return (correlation, crosslink)

def reference(ref_scan, def_scan, offsets):
    smooth, slope = tap_tables()
    smoothed = filtered(filtered(filtered(ref_scan, smooth, 2), smooth, 1), smooth, 0)
    def_gx = filtered(def_scan, smooth, 2)
    def_dx = filtered(def_scan, slope, 2)
    def_gg = filtered(def_gx, smooth, 1)
    def_dg = filtered(def_gx, slope, 1)
    def_gd = filtered(def_dx, smooth, 1)
    fields = (filtered(def_gg, smooth, 0), filtered(def_gg, slope, 0), filtered(def_dg, smooth, 0), filtered(def_gd, smooth, 0))
    slab_total = NZ // SUB
    sub_y = NY // SUB
    sub_x = NX // SUB
    volume = SUB * SUB * SUB
    cube_shape = (SUB, SUB, SUB)

    def one_subset(flat_index):
        slab_id = flat_index // (sub_y * sub_x)
        row_id = flat_index // sub_x % sub_y
        col_id = flat_index % sub_x
        corner = (slab_id * SUB, row_id * SUB, col_id * SUB)
        ref_cube = lax.dynamic_slice(smoothed, corner, cube_shape).reshape(volume)
        ref_mean = jnp.mean(ref_cube)
        centred = ref_cube - ref_mean
        normed = (centred / jnp.sqrt(jnp.sum(centred * centred) + 1e-06 * volume)).astype(jnp.bfloat16)
        current = [jnp.zeros((), jnp.float32) for index_a in range(3)]
        for turn_index in range(ITERS):
            moved_now = offsets[turn_index, :, slab_id, row_id, col_id]
            start = (corner[0] + moved_now[0], corner[1] + moved_now[1], corner[2] + moved_now[2])
            window = jnp.stack([lax.dynamic_slice(values, start, cube_shape).reshape(volume) for values in fields])
            stacked = jnp.concatenate([jnp.ones((1, volume), jnp.float32), normed.astype(jnp.float32)[None], window], axis=0)
            gram_mat = jnp.dot(stacked, stacked.T, precision=lax.Precision.HIGHEST, preferred_element_type=jnp.float32)
            newest, moment_set = gauss_newton(gram_mat, current)
            if turn_index + 1 < ITERS:
                moved_next = offsets[turn_index + 1, :, slab_id, row_id, col_id]
                current = [newest[index_a] + moved_now[index_a].astype(jnp.float32) - moved_next[index_a].astype(jnp.float32) for index_a in range(3)]
        correlation, crosslink = finish(gram_mat, newest, moment_set, ref_mean)
        return (jnp.stack(newest), correlation, crosslink)
    total_subsets = slab_total * sub_y * sub_x
    shifts, correlation, crosslink = lax.map(one_subset, jnp.arange(total_subsets, dtype=jnp.int32))
    subset_shift = shifts.T.reshape(3, slab_total, sub_y, sub_x)
    return (subset_shift, correlation.reshape(slab_total, sub_y, sub_x), crosslink.reshape(slab_total, sub_y, sub_x))
```

```python
import math

import jax
import jax.numpy as jnp
from jax import lax
from jax.experimental import pallas as pl
from jax.experimental.pallas import tpu as pltpu
from jax.sharding import PartitionSpec as P

SUB = 32
RIM = 4
JIT = 2
ITERS = 3


def extended(shard, sides, width):
    for axis, dim in sides:
        peers, length = (lax.axis_size(axis), shard.shape[dim])
        up = [(i, (i + 1) % peers) for i in range(peers - 1)]
        down = [(j, i) for i, j in up]
        last = lax.slice_in_dim(shard, length - width, length, axis=dim)
        first = lax.slice_in_dim(shard, 0, width, axis=dim)
        before = lax.ppermute(last, axis, up)
        after = lax.ppermute(first, axis, down)
        shard = jnp.concatenate([before, shard, after], axis=dim)
    return shard


def from_behind(shard, axis, by):
    peers = lax.axis_size(axis)
    pairs = [(i, i + by) for i in range(peers) if 0 <= i + by < peers]
    return lax.ppermute(shard, axis, pairs)


def tap_tables():
    spots = [float(t) for t in range(-RIM, RIM + 1)]
    bell_curve = [math.exp(-t * t / 4.5) for t in spots]
    bell_total = sum(bell_curve)
    slope_norm = sum([t * t * b for t, b in zip(spots, bell_curve)])
    smooth = [b / bell_total for b in bell_curve]
    slope = [t * b / slope_norm for t, b in zip(spots, bell_curve)]
    return (smooth, slope)


def tap_sum(padded, weights, which_axis, length):
    running = weights[0] * lax.slice_in_dim(padded, 0, length, axis=which_axis)
    for tap_index in range(1, len(weights)):
        running = running + weights[tap_index] * lax.slice_in_dim(
            padded, tap_index, tap_index + length, axis=which_axis
        )
    return running


def zero_pad(values, which_axis):
    widths = [(0, 0)] * values.ndim
    widths[which_axis] = (RIM, RIM)
    return jnp.pad(values, widths)


def solve_three(k_mat, rhs_vec):
    k_zz, k_zy, k_zx = (k_mat[0][0], k_mat[0][1], k_mat[0][2])
    k_yy, k_yx, k_xx = (k_mat[1][1], k_mat[1][2], k_mat[2][2])
    c_zz = k_yy * k_xx - k_yx * k_yx
    c_zy = k_zx * k_yx - k_zy * k_xx
    c_zx = k_zy * k_yx - k_yy * k_zx
    c_yy = k_zz * k_xx - k_zx * k_zx
    c_yx = k_zy * k_zx - k_zz * k_yx
    c_xx = k_zz * k_yy - k_zy * k_zy
    determ = k_zz * c_zz + k_zy * c_zy + k_zx * c_zx
    return [
        (c_zz * rhs_vec[0] + c_zy * rhs_vec[1] + c_zx * rhs_vec[2]) / determ,
        (c_zy * rhs_vec[0] + c_yy * rhs_vec[1] + c_yx * rhs_vec[2]) / determ,
        (c_zx * rhs_vec[0] + c_yx * rhs_vec[1] + c_xx * rhs_vec[2]) / determ,
    ]


def spread_of(centred_sq, cross_vec, k_mat, along, volume):
    square = centred_sq
    for index_a in range(3):
        square = square + 2.0 * cross_vec[index_a] * along[index_a]
        for index_b in range(3):
            square = square + along[index_a] * k_mat[index_a][index_b] * along[index_b]
    return jnp.sqrt(square + 1e-06 * volume)


def gauss_newton(gram_mat, current):
    volume = gram_mat[..., 0, 0]
    mean_val = gram_mat[..., 0, 2] / volume
    mean_grad = [gram_mat[..., 0, 3 + index_a] / volume for index_a in range(3)]
    centred_sq = gram_mat[..., 2, 2] - volume * mean_val * mean_val
    cross_vec = [
        gram_mat[..., 2, 3 + index_a] - volume * mean_val * mean_grad[index_a]
        for index_a in range(3)
    ]
    k_mat = [
        [
            gram_mat[..., 3 + index_a, 3 + index_b]
            - volume * mean_grad[index_a] * mean_grad[index_b]
            + (1e-06 * volume if index_a == index_b else 0.0)
            for index_b in range(3)
        ]
        for index_a in range(3)
    ]
    ref_grad = [
        gram_mat[..., 1, 3 + index_a] - mean_grad[index_a] * gram_mat[..., 0, 1]
        for index_a in range(3)
    ]
    spread_now = spread_of(centred_sq, cross_vec, k_mat, current, volume)
    first_part = solve_three(k_mat, ref_grad)
    second_part = solve_three(k_mat, cross_vec)
    newest = [spread_now * first_part[index_a] - second_part[index_a] for index_a in range(3)]
    return (newest, (mean_val, centred_sq, cross_vec, k_mat, ref_grad, volume))


def finish(gram_mat, newest, moment_set, ref_mean):
    mean_val, centred_sq, cross_vec, k_mat, ref_grad, volume = moment_set
    spread_new = spread_of(centred_sq, cross_vec, k_mat, newest, volume)
    score_sum = gram_mat[..., 1, 2] - mean_val * gram_mat[..., 0, 1]
    for index_a in range(3):
        score_sum = score_sum + ref_grad[index_a] * newest[index_a]
    correlation = score_sum / spread_new
    polymer = mean_val / (mean_val + ref_mean)
    crosslink = (
        -1000.0
        * (jnp.log(1.0 - polymer) + polymer + 0.4 * polymer * polymer)
        / (106.3 * (jnp.cbrt(polymer) - 0.5 * polymer))
    )
    return (correlation, crosslink)


def slot_plan(route_table, owners, slot_rank, holder, capacity, sub_x):
    slabs, subsets = owners.shape
    hit_mask = (
        (owners == holder)[:, None, :]
        & (slot_rank[:, None, :] == jnp.arange(capacity, dtype=jnp.int32)[None, :, None])
    ).astype(jnp.int32)
    is_valid = jnp.sum(hit_mask, axis=2) > 0
    picked = jnp.sum(hit_mask[None, None] * route_table[:, :, :, None, :], axis=4)
    index_j = jnp.arange(subsets, dtype=jnp.int32)
    row_pos = jnp.sum(hit_mask * (index_j // sub_x)[None, None, :], axis=2) * SUB
    col_pos = jnp.sum(hit_mask * (index_j % sub_x)[None, None, :], axis=2) * SUB
    home_z = (jnp.arange(slabs, dtype=jnp.int32) * SUB)[None, :, None]
    z_start = jnp.where(is_valid[None], home_z + picked[:, 0] - holder * SUB, 0)
    y_start = jnp.where(is_valid[None], row_pos[None] + picked[:, 1], 0)
    x_start = jnp.where(is_valid[None], col_pos[None] + picked[:, 2], 0) + JIT
    return (z_start, y_start, x_start)


PAIRS = [(i, j) for i in range(4) for j in range(i, 4)]
SUMS = 8 + len(PAIRS)


def sums_kernel(x_first, z_tile, z_in, y_part, y_in, field_ref, ref_ref, out_ref):
    step = pl.program_id(0)
    z_off = z_in[step]
    y_off = y_in[step]

    def plane(ix, acc):
        acc = list(acc)
        placed = pltpu.roll(ref_ref[0, ix].astype(jnp.float32), y_off, 1)
        for tile in range(SUB // 8):
            f = [field_ref[i, ix, pl.ds(z_off + 8 * tile, 8), :] for i in range(4)]
            r = placed[8 * tile : 8 * tile + 8]
            for i in range(4):
                acc[i] = acc[i] + f[i]
                acc[4 + i] = acc[4 + i] + f[i] * r
            for n, (i, j) in enumerate(PAIRS):
                acc[8 + n] = acc[8 + n] + f[i] * f[j]
        return tuple(acc)

    zero = jnp.zeros((8, 128), jnp.float32)
    acc = lax.fori_loop(0, SUB, plane, (zero,) * SUMS)
    lane = lax.broadcasted_iota(jnp.int32, (1, 128), 1)
    inside = (lane >= y_off) & (lane < y_off + SUB)
    for n in range(SUMS):
        total = jnp.sum(acc[n], axis=0, keepdims=True)
        out_ref[0, n : n + 1, :] = jnp.where(inside, total, 0.0)


def slot_sums(parts, arrived, z_start, y_start, x_start):
    slots = arrived.shape[0]
    steps = slots * ITERS
    z_all, y_all, x_all = [v.reshape(ITERS, slots).T.reshape(steps) for v in (z_start, y_start, x_start)]
    z_tile = jnp.minimum(z_all // 8, 3)
    y_part = jnp.where(y_all <= 96, 0, jnp.where(y_all >= 128, 2, 1))
    scalars = (x_all, z_tile, z_all - 8 * z_tile, y_part, y_all - 64 * y_part)
    element = pl.Element
    spec = pltpu.PrefetchScalarGridSpec(
        num_scalar_prefetch=5,
        grid=(steps,),
        in_specs=[
            pl.BlockSpec(
                (element(4), element(SUB), element(SUB + 8), element(128)),
                lambda s, x, zt, zi, yp, yi: (0, x[s], zt[s] * 8, yp[s] * 128),
            ),
            pl.BlockSpec((1, SUB, SUB, 128), lambda s, *_: (s // ITERS, 0, 0, 0)),
        ],
        out_specs=pl.BlockSpec((1, SUMS, 128), lambda s, *_: (s, 0, 0)),
    )
    sums = pl.pallas_call(
        sums_kernel,
        grid_spec=spec,
        out_shape=jax.ShapeDtypeStruct((steps, SUMS, 128), jnp.float32),
        compiler_params=pltpu.CompilerParams(vmem_limit_bytes=32 * 1024 * 1024),
    )(*scalars, parts, arrived)
    return jnp.sum(sums, axis=2).reshape(slots, ITERS * SUMS)


def gram_of(sums, ref_total, ref_square, volume):
    count = jnp.full(ref_total.shape, volume, jnp.float32)
    pair = {}
    for n, (i, j) in enumerate(PAIRS):
        pair[i, j] = pair[j, i] = sums[:, 8 + n]
    rows = [
        [count, ref_total] + [sums[:, i] for i in range(4)],
        [ref_total, ref_square] + [sums[:, 4 + i] for i in range(4)],
    ]
    rows += [[sums[:, i], sums[:, 4 + i]] + [pair[i, j] for j in range(4)] for i in range(4)]
    return jnp.stack([jnp.stack(row, axis=-1) for row in rows], axis=-2)


def body(ref_scan, def_scan, offsets):
    smooth, slope = tap_tables()
    slabs = lax.axis_size("slab")
    me_slab = lax.axis_index("slab")
    planes, rows_all, cols_dev = ref_scan.shape
    scan_pair = jnp.stack([ref_scan, def_scan])
    grown = extended(scan_pair, (("section", 3), ("slab", 1)), RIM)
    ref_x = tap_sum(grown[0], smooth, 2, cols_dev)
    def_gx = tap_sum(grown[1], smooth, 2, cols_dev)
    def_dx = tap_sum(grown[1], slope, 2, cols_dev)
    ref_xy = tap_sum(zero_pad(ref_x, 1), smooth, 1, rows_all)
    gx_pad = zero_pad(def_gx, 1)
    def_gg = tap_sum(gx_pad, smooth, 1, rows_all)
    def_dg = tap_sum(gx_pad, slope, 1, rows_all)
    def_gd = tap_sum(zero_pad(def_dx, 1), smooth, 1, rows_all)
    smoothed = tap_sum(ref_xy, smooth, 0, planes)
    fields = jnp.stack(
        [
            tap_sum(def_gg, smooth, 0, planes),
            tap_sum(def_gg, slope, 0, planes),
            tap_sum(def_dg, smooth, 0, planes),
            tap_sum(def_gd, smooth, 0, planes),
        ]
    )
    fields_wide = extended(fields, (("section", 3),), JIT)
    sub_y = rows_all // SUB
    sub_x = cols_dev // SUB
    subsets = sub_y * sub_x
    volume = SUB * SUB * SUB
    blocks = (
        smoothed.reshape(SUB, sub_y, SUB, sub_x, SUB)
        .transpose(1, 3, 4, 0, 2)
        .reshape(subsets, volume)
    )
    ref_mean = jnp.mean(blocks, axis=1)
    centred = blocks - ref_mean[:, None]
    normed = (
        centred / jnp.sqrt(jnp.sum(centred * centred, axis=1) + 1e-06 * volume)[:, None]
    ).astype(jnp.bfloat16)
    route_table = offsets.reshape(ITERS, 3, slabs, subsets)
    owners = (jnp.arange(slabs, dtype=jnp.int32)[:, None] * SUB + route_table[0, 0]) // SUB
    earlier = (
        jnp.arange(subsets, dtype=jnp.int32)[:, None]
        > jnp.arange(subsets, dtype=jnp.int32)[None, :]
    )
    same_slab = owners[:, :, None] == owners[:, None, :]
    slot_rank = jnp.sum(same_slab & earlier[None], axis=2)
    capacity = max(2, (subsets + slabs - 1) // slabs)
    my_owner = lax.dynamic_index_in_dim(owners, me_slab, 0, keepdims=False)
    my_rank = lax.dynamic_index_in_dim(slot_rank, me_slab, 0, keepdims=False)
    outgoing = jnp.zeros((slabs, capacity, volume), jnp.bfloat16).at[my_owner, my_rank].set(normed)
    arrived = lax.all_to_all(outgoing, "slab", split_axis=0, concat_axis=0, tiled=True)
    plan_own = slot_plan(route_table, owners, slot_rank, me_slab, capacity, sub_x)
    turned = fields_wide.transpose(0, 3, 1, 2)
    half = rows_all // 4
    beyond = from_behind(turned, "slab", -1)
    tall = jnp.concatenate([turned, beyond], axis=2)
    parts = jnp.concatenate(
        [tall[..., :128], tall[..., half : half + 128], tall[..., 128:]], axis=3
    )
    cubes = arrived.reshape(slabs * capacity, SUB, SUB, SUB)
    cubes = jnp.concatenate([cubes] * 4, axis=3)
    ref_total = jnp.sum(normed.astype(jnp.float32), axis=1)
    ref_square = jnp.sum(normed.astype(jnp.float32) ** 2, axis=1)
    sums = slot_sums(parts, cubes, *plan_own)
    returned = lax.all_to_all(
        sums.reshape(slabs, capacity, ITERS * SUMS), "slab", split_axis=0, concat_axis=0, tiled=True
    )
    mine = returned[my_owner, my_rank].reshape(subsets, ITERS, SUMS)
    my_table = lax.dynamic_index_in_dim(route_table, me_slab, 2, keepdims=False).astype(jnp.float32)
    current = [jnp.zeros((subsets,), jnp.float32) for index_a in range(3)]
    for turn_index in range(ITERS):
        my_grams = gram_of(mine[:, turn_index], ref_total, ref_square, float(volume))
        newest, moment_set = gauss_newton(my_grams, current)
        if turn_index + 1 < ITERS:
            current = [
                newest[index_a] + my_table[turn_index, index_a] - my_table[turn_index + 1, index_a]
                for index_a in range(3)
            ]
    correlation, crosslink = finish(my_grams, newest, moment_set, ref_mean)
    subset_shift = jnp.stack(newest).reshape(3, 1, sub_y, sub_x)
    return (subset_shift, correlation.reshape(1, sub_y, sub_x), crosslink.reshape(1, sub_y, sub_x))


def solution(mesh):
    in_specs = (
        P("slab", None, "section"),
        P("slab", None, "section"),
        P(None, None, None, None, "section"),
    )
    out_specs = (
        P(None, "slab", None, "section"),
        P("slab", None, "section"),
        P("slab", None, "section"),
    )
    return jax.shard_map(body, mesh=mesh, in_specs=in_specs, out_specs=out_specs, check_vma=False)
```

```python
import math

import jax
import jax.numpy as jnp
import numpy as np
from jax import lax
from jax.experimental import pallas as pl
from jax.experimental.pallas import tpu as pltpu
from jax.sharding import PartitionSpec as P

SUB = 32
RIM = 4
JIT = 2
ITERS = 3


def extended(shard, sides, width):
    for axis, dim in sides:
        peers, length = (lax.axis_size(axis), shard.shape[dim])
        up = [(i, (i + 1) % peers) for i in range(peers - 1)]
        down = [(j, i) for i, j in up]
        last = lax.slice_in_dim(shard, length - width, length, axis=dim)
        first = lax.slice_in_dim(shard, 0, width, axis=dim)
        before = lax.ppermute(last, axis, up)
        after = lax.ppermute(first, axis, down)
        shard = jnp.concatenate([before, shard, after], axis=dim)
    return shard


def from_behind(shard, axis, by):
    peers = lax.axis_size(axis)
    pairs = [(i, i + by) for i in range(peers) if 0 <= i + by < peers]
    return lax.ppermute(shard, axis, pairs)


def tap_tables():
    spots = [float(t) for t in range(-RIM, RIM + 1)]
    bell_curve = [math.exp(-t * t / 4.5) for t in spots]
    bell_total = sum(bell_curve)
    slope_norm = sum([t * t * b for t, b in zip(spots, bell_curve)])
    smooth = [b / bell_total for b in bell_curve]
    slope = [t * b / slope_norm for t, b in zip(spots, bell_curve)]
    return (smooth, slope)


def tap_sum(padded, weights, which_axis, length):
    running = weights[0] * lax.slice_in_dim(padded, 0, length, axis=which_axis)
    for tap_index in range(1, len(weights)):
        running = running + weights[tap_index] * lax.slice_in_dim(
            padded, tap_index, tap_index + length, axis=which_axis
        )
    return running


def rows_filtered(values, weights):
    rows = values.shape[1]
    band = jnp.asarray(
        sum(w * np.eye(rows, k=RIM - t) for t, w in enumerate(weights)), jnp.float32
    )
    planes, _, cols = values.shape
    lines = values.transpose(2, 0, 1).reshape(cols * planes, rows)
    done = jnp.dot(
        lines, band, precision=lax.Precision.HIGHEST, preferred_element_type=jnp.float32
    )
    return done.reshape(cols, planes, rows).transpose(1, 2, 0)


def solve_three(k_mat, rhs_vec):
    k_zz, k_zy, k_zx = (k_mat[0][0], k_mat[0][1], k_mat[0][2])
    k_yy, k_yx, k_xx = (k_mat[1][1], k_mat[1][2], k_mat[2][2])
    c_zz = k_yy * k_xx - k_yx * k_yx
    c_zy = k_zx * k_yx - k_zy * k_xx
    c_zx = k_zy * k_yx - k_yy * k_zx
    c_yy = k_zz * k_xx - k_zx * k_zx
    c_yx = k_zy * k_zx - k_zz * k_yx
    c_xx = k_zz * k_yy - k_zy * k_zy
    determ = k_zz * c_zz + k_zy * c_zy + k_zx * c_zx
    return [
        (c_zz * rhs_vec[0] + c_zy * rhs_vec[1] + c_zx * rhs_vec[2]) / determ,
        (c_zy * rhs_vec[0] + c_yy * rhs_vec[1] + c_yx * rhs_vec[2]) / determ,
        (c_zx * rhs_vec[0] + c_yx * rhs_vec[1] + c_xx * rhs_vec[2]) / determ,
    ]


def spread_of(centred_sq, cross_vec, k_mat, along, volume):
    square = centred_sq
    for index_a in range(3):
        square = square + 2.0 * cross_vec[index_a] * along[index_a]
        for index_b in range(3):
            square = square + along[index_a] * k_mat[index_a][index_b] * along[index_b]
    return jnp.sqrt(square + 1e-06 * volume)


def gauss_newton(gram_mat, current):
    volume = gram_mat[..., 0, 0]
    mean_val = gram_mat[..., 0, 2] / volume
    mean_grad = [gram_mat[..., 0, 3 + index_a] / volume for index_a in range(3)]
    centred_sq = gram_mat[..., 2, 2] - volume * mean_val * mean_val
    cross_vec = [
        gram_mat[..., 2, 3 + index_a] - volume * mean_val * mean_grad[index_a]
        for index_a in range(3)
    ]
    k_mat = [
        [
            gram_mat[..., 3 + index_a, 3 + index_b]
            - volume * mean_grad[index_a] * mean_grad[index_b]
            + (1e-06 * volume if index_a == index_b else 0.0)
            for index_b in range(3)
        ]
        for index_a in range(3)
    ]
    ref_grad = [
        gram_mat[..., 1, 3 + index_a] - mean_grad[index_a] * gram_mat[..., 0, 1]
        for index_a in range(3)
    ]
    spread_now = spread_of(centred_sq, cross_vec, k_mat, current, volume)
    first_part = solve_three(k_mat, ref_grad)
    second_part = solve_three(k_mat, cross_vec)
    newest = [spread_now * first_part[index_a] - second_part[index_a] for index_a in range(3)]
    return (newest, (mean_val, centred_sq, cross_vec, k_mat, ref_grad, volume))


def finish(gram_mat, newest, moment_set, ref_mean):
    mean_val, centred_sq, cross_vec, k_mat, ref_grad, volume = moment_set
    spread_new = spread_of(centred_sq, cross_vec, k_mat, newest, volume)
    score_sum = gram_mat[..., 1, 2] - mean_val * gram_mat[..., 0, 1]
    for index_a in range(3):
        score_sum = score_sum + ref_grad[index_a] * newest[index_a]
    correlation = score_sum / spread_new
    polymer = mean_val / (mean_val + ref_mean)
    crosslink = (
        -1000.0
        * (jnp.log(1.0 - polymer) + polymer + 0.4 * polymer * polymer)
        / (106.3 * (jnp.cbrt(polymer) - 0.5 * polymer))
    )
    return (correlation, crosslink)


def slot_plan(route_table, owners, slot_rank, holder, capacity, sub_x):
    slabs, subsets = owners.shape
    hit_mask = (
        (owners == holder)[:, None, :]
        & (slot_rank[:, None, :] == jnp.arange(capacity, dtype=jnp.int32)[None, :, None])
    ).astype(jnp.int32)
    is_valid = jnp.sum(hit_mask, axis=2) > 0
    picked = jnp.sum(hit_mask[None, None] * route_table[:, :, :, None, :], axis=4)
    index_j = jnp.arange(subsets, dtype=jnp.int32)
    row_pos = jnp.sum(hit_mask * (index_j // sub_x)[None, None, :], axis=2) * SUB
    col_pos = jnp.sum(hit_mask * (index_j % sub_x)[None, None, :], axis=2) * SUB
    home_z = (jnp.arange(slabs, dtype=jnp.int32) * SUB)[None, :, None]
    z_start = jnp.where(is_valid[None], home_z + picked[:, 0] - holder * SUB, 0)
    y_start = jnp.where(is_valid[None], row_pos[None] + picked[:, 1], 0)
    x_start = jnp.where(is_valid[None], col_pos[None] + picked[:, 2], 0) + JIT
    return (z_start, y_start, x_start)


PAIRS = [(i, j) for i in range(4) for j in range(i, 4)]
SUMS = 8 + len(PAIRS)


def sums_kernel(x_first, z_tile, z_in, y_part, y_in, field_ref, ref_ref, out_ref):
    step = pl.program_id(0)
    z_off = z_in[step]
    y_off = y_in[step]

    def plane(ix, acc):
        acc = list(acc)
        placed = pltpu.roll(ref_ref[0, ix].astype(jnp.float32), y_off, 1)
        for tile in range(SUB // 8):
            f = [field_ref[0, i, ix, pl.ds(z_off + 8 * tile, 8), :] for i in range(4)]
            r = placed[8 * tile : 8 * tile + 8]
            for i in range(4):
                acc[i] = acc[i] + f[i]
                acc[4 + i] = acc[4 + i] + f[i] * r
            for n, (i, j) in enumerate(PAIRS):
                acc[8 + n] = acc[8 + n] + f[i] * f[j]
        return tuple(acc)

    zero = jnp.zeros((8, 128), jnp.float32)
    acc = lax.fori_loop(0, SUB, plane, (zero,) * SUMS, unroll=4)
    lane = lax.broadcasted_iota(jnp.int32, (1, 128), 1)
    inside = (lane >= y_off) & (lane < y_off + SUB)
    for n in range(SUMS):
        total = jnp.sum(acc[n], axis=0, keepdims=True)
        out_ref[0, n : n + 1, :] = jnp.where(inside, total, 0.0)


def slot_sums(parts, arrived, z_start, y_start, x_start):
    slots = arrived.shape[0]
    steps = slots * ITERS
    z_all, y_all, x_all = [v.reshape(ITERS, slots).T.reshape(steps) for v in (z_start, y_start, x_start)]
    z_tile = jnp.minimum(z_all // 8, 3)
    y_part = jnp.where(y_all <= 96, 0, jnp.where(y_all >= 128, 2, 1))
    scalars = (x_all, z_tile, z_all - 8 * z_tile, y_part, y_all - 64 * y_part)
    element = pl.Element
    spec = pltpu.PrefetchScalarGridSpec(
        num_scalar_prefetch=5,
        grid=(steps,),
        in_specs=[
            pl.BlockSpec(
                (element(1), element(4), element(SUB), element(SUB + 8), element(128)),
                lambda s, x, zt, zi, yp, yi: (yp[s], 0, x[s], zt[s] * 8, 0),
            ),
            pl.BlockSpec((1, SUB, SUB, 128), lambda s, *_: (s // ITERS, 0, 0, 0)),
        ],
        out_specs=pl.BlockSpec((1, SUMS, 128), lambda s, *_: (s, 0, 0)),
    )
    sums = pl.pallas_call(
        sums_kernel,
        grid_spec=spec,
        out_shape=jax.ShapeDtypeStruct((steps, SUMS, 128), jnp.float32),
        compiler_params=pltpu.CompilerParams(vmem_limit_bytes=32 * 1024 * 1024),
    )(*scalars, parts, arrived)
    return jnp.sum(sums, axis=2).reshape(slots, ITERS * SUMS)


def gram_of(sums, ref_total, ref_square, volume):
    count = jnp.full(ref_total.shape, volume, jnp.float32)
    pair = {}
    for n, (i, j) in enumerate(PAIRS):
        pair[i, j] = pair[j, i] = sums[:, 8 + n]
    rows = [
        [count, ref_total] + [sums[:, i] for i in range(4)],
        [ref_total, ref_square] + [sums[:, 4 + i] for i in range(4)],
    ]
    rows += [[sums[:, i], sums[:, 4 + i]] + [pair[i, j] for j in range(4)] for i in range(4)]
    return jnp.stack([jnp.stack(row, axis=-1) for row in rows], axis=-2)


def body(ref_scan, def_scan, offsets):
    smooth, slope = tap_tables()
    slabs = lax.axis_size("slab")
    me_slab = lax.axis_index("slab")
    planes, rows_all, cols_dev = ref_scan.shape
    scan_pair = jnp.stack([ref_scan, def_scan])
    grown = extended(scan_pair, (("section", 3), ("slab", 1)), RIM)
    ref_x = tap_sum(grown[0], smooth, 2, cols_dev)
    def_gx = tap_sum(grown[1], smooth, 2, cols_dev)
    def_dx = tap_sum(grown[1], slope, 2, cols_dev)
    ref_xy = rows_filtered(ref_x, smooth)
    def_gg = rows_filtered(def_gx, smooth)
    def_dg = rows_filtered(def_gx, slope)
    def_gd = rows_filtered(def_dx, smooth)
    smoothed = tap_sum(ref_xy, smooth, 0, planes)
    fields = jnp.stack(
        [
            tap_sum(def_gg, smooth, 0, planes),
            tap_sum(def_gg, slope, 0, planes),
            tap_sum(def_dg, smooth, 0, planes),
            tap_sum(def_gd, smooth, 0, planes),
        ]
    )
    fields_wide = extended(fields, (("section", 3),), JIT)
    sub_y = rows_all // SUB
    sub_x = cols_dev // SUB
    subsets = sub_y * sub_x
    volume = SUB * SUB * SUB
    blocks = (
        smoothed.reshape(SUB, sub_y, SUB, sub_x, SUB)
        .transpose(1, 3, 4, 0, 2)
        .reshape(subsets, volume)
    )
    ref_mean = jnp.mean(blocks, axis=1)
    centred = blocks - ref_mean[:, None]
    normed = (
        centred / jnp.sqrt(jnp.sum(centred * centred, axis=1) + 1e-06 * volume)[:, None]
    ).astype(jnp.bfloat16)
    route_table = offsets.reshape(ITERS, 3, slabs, subsets)
    owners = (jnp.arange(slabs, dtype=jnp.int32)[:, None] * SUB + route_table[0, 0]) // SUB
    earlier = (
        jnp.arange(subsets, dtype=jnp.int32)[:, None]
        > jnp.arange(subsets, dtype=jnp.int32)[None, :]
    )
    same_slab = owners[:, :, None] == owners[:, None, :]
    slot_rank = jnp.sum(same_slab & earlier[None], axis=2)
    capacity = max(2, (subsets + slabs - 1) // slabs)
    my_owner = lax.dynamic_index_in_dim(owners, me_slab, 0, keepdims=False)
    my_rank = lax.dynamic_index_in_dim(slot_rank, me_slab, 0, keepdims=False)
    my_slot = my_owner * capacity + my_rank
    chosen = (
        jnp.arange(slabs * capacity, dtype=jnp.int32)[:, None] == my_slot[None, :]
    ).astype(jnp.bfloat16)
    outgoing = jnp.dot(chosen, normed, preferred_element_type=jnp.float32)
    outgoing = outgoing.astype(jnp.bfloat16).reshape(slabs, capacity, volume)
    arrived = lax.all_to_all(outgoing, "slab", split_axis=0, concat_axis=0, tiled=True)
    plan_own = slot_plan(route_table, owners, slot_rank, me_slab, capacity, sub_x)
    turned = fields_wide.transpose(0, 3, 1, 2)
    half = rows_all // 4
    beyond = from_behind(turned, "slab", -1)
    tall = jnp.concatenate([turned, beyond], axis=2)
    parts = jnp.stack([tall[..., :128], tall[..., half : half + 128], tall[..., 128:]])
    cubes = arrived.reshape(slabs * capacity, SUB, SUB, SUB)
    cubes = jnp.concatenate([cubes] * 4, axis=3)
    ref_total = jnp.sum(normed.astype(jnp.float32), axis=1)
    ref_square = jnp.sum(normed.astype(jnp.float32) ** 2, axis=1)
    sums = slot_sums(parts, cubes, *plan_own)
    returned = lax.all_to_all(
        sums.reshape(slabs, capacity, ITERS * SUMS), "slab", split_axis=0, concat_axis=0, tiled=True
    )
    mine = returned[my_owner, my_rank].reshape(subsets, ITERS, SUMS)
    my_table = lax.dynamic_index_in_dim(route_table, me_slab, 2, keepdims=False).astype(jnp.float32)
    current = [jnp.zeros((subsets,), jnp.float32) for index_a in range(3)]
    for turn_index in range(ITERS):
        my_grams = gram_of(mine[:, turn_index], ref_total, ref_square, float(volume))
        newest, moment_set = gauss_newton(my_grams, current)
        if turn_index + 1 < ITERS:
            current = [
                newest[index_a] + my_table[turn_index, index_a] - my_table[turn_index + 1, index_a]
                for index_a in range(3)
            ]
    correlation, crosslink = finish(my_grams, newest, moment_set, ref_mean)
    subset_shift = jnp.stack(newest).reshape(3, 1, sub_y, sub_x)
    return (subset_shift, correlation.reshape(1, sub_y, sub_x), crosslink.reshape(1, sub_y, sub_x))


def solution(mesh):
    in_specs = (
        P("slab", None, "section"),
        P("slab", None, "section"),
        P(None, None, None, None, "section"),
    )
    out_specs = (
        P(None, "slab", None, "section"),
        P("slab", None, "section"),
        P("slab", None, "section"),
    )
    return jax.shard_map(body, mesh=mesh, in_specs=in_specs, out_specs=out_specs, check_vma=False)
```

```python
import math

import jax
import jax.numpy as jnp
import numpy as np
from jax import lax
from jax.experimental import pallas as pl
from jax.experimental.pallas import tpu as pltpu
from jax.sharding import PartitionSpec as P

SUB = 32
RIM = 4
JIT = 2
ITERS = 3


def extended(shard, sides, width):
    for axis, dim in sides:
        peers, length = (lax.axis_size(axis), shard.shape[dim])
        up = [(i, (i + 1) % peers) for i in range(peers - 1)]
        down = [(j, i) for i, j in up]
        last = lax.slice_in_dim(shard, length - width, length, axis=dim)
        first = lax.slice_in_dim(shard, 0, width, axis=dim)
        before = lax.ppermute(last, axis, up)
        after = lax.ppermute(first, axis, down)
        shard = jnp.concatenate([before, shard, after], axis=dim)
    return shard


def from_behind(shard, axis, by):
    peers = lax.axis_size(axis)
    pairs = [(i, i + by) for i in range(peers) if 0 <= i + by < peers]
    return lax.ppermute(shard, axis, pairs)


def tap_tables():
    spots = [float(t) for t in range(-RIM, RIM + 1)]
    bell_curve = [math.exp(-t * t / 4.5) for t in spots]
    bell_total = sum(bell_curve)
    slope_norm = sum([t * t * b for t, b in zip(spots, bell_curve)])
    smooth = [b / bell_total for b in bell_curve]
    slope = [t * b / slope_norm for t, b in zip(spots, bell_curve)]
    return (smooth, slope)


def tap_sum(padded, weights, which_axis, length):
    running = weights[0] * lax.slice_in_dim(padded, 0, length, axis=which_axis)
    for tap_index in range(1, len(weights)):
        running = running + weights[tap_index] * lax.slice_in_dim(
            padded, tap_index, tap_index + length, axis=which_axis
        )
    return running


def rows_filtered(values, weights):
    rows = values.shape[1]
    band = jnp.asarray(
        sum(w * np.eye(rows, k=RIM - t) for t, w in enumerate(weights)), jnp.float32
    )
    planes, _, cols = values.shape
    lines = values.transpose(2, 0, 1).reshape(cols * planes, rows)
    done = jnp.dot(
        lines, band, precision=lax.Precision.HIGHEST, preferred_element_type=jnp.float32
    )
    return done.reshape(cols, planes, rows).transpose(1, 2, 0)


def solve_three(k_mat, rhs_vec):
    k_zz, k_zy, k_zx = (k_mat[0][0], k_mat[0][1], k_mat[0][2])
    k_yy, k_yx, k_xx = (k_mat[1][1], k_mat[1][2], k_mat[2][2])
    c_zz = k_yy * k_xx - k_yx * k_yx
    c_zy = k_zx * k_yx - k_zy * k_xx
    c_zx = k_zy * k_yx - k_yy * k_zx
    c_yy = k_zz * k_xx - k_zx * k_zx
    c_yx = k_zy * k_zx - k_zz * k_yx
    c_xx = k_zz * k_yy - k_zy * k_zy
    determ = k_zz * c_zz + k_zy * c_zy + k_zx * c_zx
    return [
        (c_zz * rhs_vec[0] + c_zy * rhs_vec[1] + c_zx * rhs_vec[2]) / determ,
        (c_zy * rhs_vec[0] + c_yy * rhs_vec[1] + c_yx * rhs_vec[2]) / determ,
        (c_zx * rhs_vec[0] + c_yx * rhs_vec[1] + c_xx * rhs_vec[2]) / determ,
    ]


def spread_of(centred_sq, cross_vec, k_mat, along, volume):
    square = centred_sq
    for index_a in range(3):
        square = square + 2.0 * cross_vec[index_a] * along[index_a]
        for index_b in range(3):
            square = square + along[index_a] * k_mat[index_a][index_b] * along[index_b]
    return jnp.sqrt(square + 1e-06 * volume)


def gauss_newton(gram_mat, current):
    volume = gram_mat[..., 0, 0]
    mean_val = gram_mat[..., 0, 2] / volume
    mean_grad = [gram_mat[..., 0, 3 + index_a] / volume for index_a in range(3)]
    centred_sq = gram_mat[..., 2, 2] - volume * mean_val * mean_val
    cross_vec = [
        gram_mat[..., 2, 3 + index_a] - volume * mean_val * mean_grad[index_a]
        for index_a in range(3)
    ]
    k_mat = [
        [
            gram_mat[..., 3 + index_a, 3 + index_b]
            - volume * mean_grad[index_a] * mean_grad[index_b]
            + (1e-06 * volume if index_a == index_b else 0.0)
            for index_b in range(3)
        ]
        for index_a in range(3)
    ]
    ref_grad = [
        gram_mat[..., 1, 3 + index_a] - mean_grad[index_a] * gram_mat[..., 0, 1]
        for index_a in range(3)
    ]
    spread_now = spread_of(centred_sq, cross_vec, k_mat, current, volume)
    first_part = solve_three(k_mat, ref_grad)
    second_part = solve_three(k_mat, cross_vec)
    newest = [spread_now * first_part[index_a] - second_part[index_a] for index_a in range(3)]
    return (newest, (mean_val, centred_sq, cross_vec, k_mat, ref_grad, volume))


def finish(gram_mat, newest, moment_set, ref_mean):
    mean_val, centred_sq, cross_vec, k_mat, ref_grad, volume = moment_set
    spread_new = spread_of(centred_sq, cross_vec, k_mat, newest, volume)
    score_sum = gram_mat[..., 1, 2] - mean_val * gram_mat[..., 0, 1]
    for index_a in range(3):
        score_sum = score_sum + ref_grad[index_a] * newest[index_a]
    correlation = score_sum / spread_new
    polymer = mean_val / (mean_val + ref_mean)
    crosslink = (
        -1000.0
        * (jnp.log(1.0 - polymer) + polymer + 0.4 * polymer * polymer)
        / (106.3 * (jnp.cbrt(polymer) - 0.5 * polymer))
    )
    return (correlation, crosslink)


def slot_plan(route_table, owners, slot_rank, holder, capacity, sub_x):
    slabs, subsets = owners.shape
    hit_mask = (
        (owners == holder)[:, None, :]
        & (slot_rank[:, None, :] == jnp.arange(capacity, dtype=jnp.int32)[None, :, None])
    ).astype(jnp.int32)
    is_valid = jnp.sum(hit_mask, axis=2) > 0
    picked = jnp.sum(hit_mask[None, None] * route_table[:, :, :, None, :], axis=4)
    index_j = jnp.arange(subsets, dtype=jnp.int32)
    row_pos = jnp.sum(hit_mask * (index_j // sub_x)[None, None, :], axis=2) * SUB
    col_pos = jnp.sum(hit_mask * (index_j % sub_x)[None, None, :], axis=2) * SUB
    home_z = (jnp.arange(slabs, dtype=jnp.int32) * SUB)[None, :, None]
    z_start = jnp.where(is_valid[None], home_z + picked[:, 0] - holder * SUB, 0)
    y_start = jnp.where(is_valid[None], row_pos[None] + picked[:, 1], 0)
    x_start = jnp.where(is_valid[None], col_pos[None] + picked[:, 2], 0) + JIT
    return (z_start, y_start, x_start)


PAIRS = [(i, j) for i in range(4) for j in range(i, 4)]
SUMS = 8 + len(PAIRS)


def sums_kernel(x_first, z_tile, z_in, y_part, y_in, field_ref, ref_ref, out_ref):
    step = pl.program_id(0)
    z_off = z_in[step]
    y_off = y_in[step]

    def plane(ix, acc):
        acc = list(acc)
        placed = pltpu.roll(ref_ref[0, ix].astype(jnp.float32), y_off, 1)
        for tile in range(SUB // 8):
            f = [field_ref[0, i, ix, pl.ds(z_off + 8 * tile, 8), :] for i in range(4)]
            r = placed[8 * tile : 8 * tile + 8]
            for i in range(4):
                acc[i] = acc[i] + f[i]
                acc[4 + i] = acc[4 + i] + f[i] * r
            for n, (i, j) in enumerate(PAIRS):
                acc[8 + n] = acc[8 + n] + f[i] * f[j]
        return tuple(acc)

    zero = jnp.zeros((8, 128), jnp.float32)
    acc = lax.fori_loop(0, SUB, plane, (zero,) * SUMS, unroll=8)
    lane = lax.broadcasted_iota(jnp.int32, (1, 128), 1)
    inside = (lane >= y_off) & (lane < y_off + SUB)
    for n in range(SUMS):
        total = jnp.sum(acc[n], axis=0, keepdims=True)
        out_ref[0, n : n + 1, :] = jnp.where(inside, total, 0.0)


def slot_sums(parts, arrived, z_start, y_start, x_start):
    slots = arrived.shape[0]
    steps = slots * ITERS
    z_all, y_all, x_all = [v.reshape(ITERS, slots).T.reshape(steps) for v in (z_start, y_start, x_start)]
    z_tile = jnp.minimum(z_all // 8, 3)
    y_part = jnp.where(y_all <= 96, 0, jnp.where(y_all >= 128, 2, 1))
    scalars = (x_all, z_tile, z_all - 8 * z_tile, y_part, y_all - 64 * y_part)
    element = pl.Element
    spec = pltpu.PrefetchScalarGridSpec(
        num_scalar_prefetch=5,
        grid=(steps,),
        in_specs=[
            pl.BlockSpec(
                (element(1), element(4), element(SUB), element(SUB + 8), element(128)),
                lambda s, x, zt, zi, yp, yi: (yp[s], 0, x[s], zt[s] * 8, 0),
            ),
            pl.BlockSpec((1, SUB, SUB, 128), lambda s, *_: (s // ITERS, 0, 0, 0)),
        ],
        out_specs=pl.BlockSpec((1, SUMS, 128), lambda s, *_: (s, 0, 0)),
    )
    sums = pl.pallas_call(
        sums_kernel,
        grid_spec=spec,
        out_shape=jax.ShapeDtypeStruct((steps, SUMS, 128), jnp.float32),
        compiler_params=pltpu.CompilerParams(vmem_limit_bytes=32 * 1024 * 1024),
    )(*scalars, parts, arrived)
    return jnp.sum(sums, axis=2).reshape(slots, ITERS * SUMS)


def gram_of(sums, ref_total, ref_square, volume):
    count = jnp.full(ref_total.shape, volume, jnp.float32)
    pair = {}
    for n, (i, j) in enumerate(PAIRS):
        pair[i, j] = pair[j, i] = sums[:, 8 + n]
    rows = [
        [count, ref_total] + [sums[:, i] for i in range(4)],
        [ref_total, ref_square] + [sums[:, 4 + i] for i in range(4)],
    ]
    rows += [[sums[:, i], sums[:, 4 + i]] + [pair[i, j] for j in range(4)] for i in range(4)]
    return jnp.stack([jnp.stack(row, axis=-1) for row in rows], axis=-2)


def body(ref_scan, def_scan, offsets):
    smooth, slope = tap_tables()
    slabs = lax.axis_size("slab")
    me_slab = lax.axis_index("slab")
    planes, rows_all, cols_dev = ref_scan.shape
    scan_pair = jnp.stack([ref_scan, def_scan])
    grown = extended(scan_pair, (("section", 3), ("slab", 1)), RIM)
    ref_x = tap_sum(grown[0], smooth, 2, cols_dev)
    def_gx = tap_sum(grown[1], smooth, 2, cols_dev)
    def_dx = tap_sum(grown[1], slope, 2, cols_dev)
    ref_xy = rows_filtered(ref_x, smooth)
    def_gg = rows_filtered(def_gx, smooth)
    def_dg = rows_filtered(def_gx, slope)
    def_gd = rows_filtered(def_dx, smooth)
    smoothed = tap_sum(ref_xy, smooth, 0, planes)
    fields = jnp.stack(
        [
            tap_sum(def_gg, smooth, 0, planes),
            tap_sum(def_gg, slope, 0, planes),
            tap_sum(def_dg, smooth, 0, planes),
            tap_sum(def_gd, smooth, 0, planes),
        ]
    )
    fields_wide = extended(fields, (("section", 3),), JIT)
    sub_y = rows_all // SUB
    sub_x = cols_dev // SUB
    subsets = sub_y * sub_x
    volume = SUB * SUB * SUB
    blocks = (
        smoothed.reshape(SUB, sub_y, SUB, sub_x, SUB)
        .transpose(1, 3, 4, 0, 2)
        .reshape(subsets, volume)
    )
    ref_mean = jnp.mean(blocks, axis=1)
    centred = blocks - ref_mean[:, None]
    normed = (
        centred / jnp.sqrt(jnp.sum(centred * centred, axis=1) + 1e-06 * volume)[:, None]
    ).astype(jnp.bfloat16)
    route_table = offsets.reshape(ITERS, 3, slabs, subsets)
    owners = (jnp.arange(slabs, dtype=jnp.int32)[:, None] * SUB + route_table[0, 0]) // SUB
    earlier = (
        jnp.arange(subsets, dtype=jnp.int32)[:, None]
        > jnp.arange(subsets, dtype=jnp.int32)[None, :]
    )
    same_slab = owners[:, :, None] == owners[:, None, :]
    slot_rank = jnp.sum(same_slab & earlier[None], axis=2)
    capacity = max(2, (subsets + slabs - 1) // slabs)
    my_owner = lax.dynamic_index_in_dim(owners, me_slab, 0, keepdims=False)
    my_rank = lax.dynamic_index_in_dim(slot_rank, me_slab, 0, keepdims=False)
    my_slot = my_owner * capacity + my_rank
    chosen = (
        jnp.arange(slabs * capacity, dtype=jnp.int32)[:, None] == my_slot[None, :]
    ).astype(jnp.bfloat16)
    outgoing = jnp.dot(chosen, normed, preferred_element_type=jnp.float32)
    outgoing = outgoing.astype(jnp.bfloat16).reshape(slabs, capacity, volume)
    arrived = lax.all_to_all(outgoing, "slab", split_axis=0, concat_axis=0, tiled=True)
    plan_own = slot_plan(route_table, owners, slot_rank, me_slab, capacity, sub_x)
    turned = fields_wide.transpose(0, 3, 1, 2)
    half = rows_all // 4
    beyond = from_behind(turned, "slab", -1)
    tall = jnp.concatenate([turned, beyond], axis=2)
    parts = jnp.stack([tall[..., :128], tall[..., half : half + 128], tall[..., 128:]])
    cubes = arrived.reshape(slabs * capacity, SUB, SUB, SUB)
    cubes = jnp.concatenate([cubes] * 4, axis=3)
    ref_total = jnp.sum(normed.astype(jnp.float32), axis=1)
    ref_square = jnp.sum(normed.astype(jnp.float32) ** 2, axis=1)
    sums = slot_sums(parts, cubes, *plan_own)
    returned = lax.all_to_all(
        sums.reshape(slabs, capacity, ITERS * SUMS), "slab", split_axis=0, concat_axis=0, tiled=True
    )
    mine = returned[my_owner, my_rank].reshape(subsets, ITERS, SUMS)
    my_table = lax.dynamic_index_in_dim(route_table, me_slab, 2, keepdims=False).astype(jnp.float32)
    current = [jnp.zeros((subsets,), jnp.float32) for index_a in range(3)]
    for turn_index in range(ITERS):
        my_grams = gram_of(mine[:, turn_index], ref_total, ref_square, float(volume))
        newest, moment_set = gauss_newton(my_grams, current)
        if turn_index + 1 < ITERS:
            current = [
                newest[index_a] + my_table[turn_index, index_a] - my_table[turn_index + 1, index_a]
                for index_a in range(3)
            ]
    correlation, crosslink = finish(my_grams, newest, moment_set, ref_mean)
    subset_shift = jnp.stack(newest).reshape(3, 1, sub_y, sub_x)
    return (subset_shift, correlation.reshape(1, sub_y, sub_x), crosslink.reshape(1, sub_y, sub_x))


def solution(mesh):
    in_specs = (
        P("slab", None, "section"),
        P("slab", None, "section"),
        P(None, None, None, None, "section"),
    )
    out_specs = (
        P(None, "slab", None, "section"),
        P("slab", None, "section"),
        P("slab", None, "section"),
    )
    return jax.shard_map(body, mesh=mesh, in_specs=in_specs, out_specs=out_specs, check_vma=False)
```
